32 devices in a mesh: fsdp: 16 (over z, y, x), rep: 2 (over core).
Axes of the slice: x: 2, y: 2, z: 4, core: 2. Of those that a mesh axis runs over, the one named last changes fastest.
Arguments:
- statistics: float32 [32, 1024, 1024], P('fsdp'), as said below
- warm_roots: float32 [32, 1024, 1024], P('fsdp')
- orders: int32 [32], replicated, may hold values from 512 to 1024, as said below
Outputs:
- roots: float32 [32, 1024, 1024], P('fsdp')
The draws below stay inside these ranges and needn't reach their ends.
Inputs may be any that keep to these rules, and one draw needn't show every extreme that they name: `orders`: each order is 512 plus a multiple of 128. `statistics`: symmetric in its last two dimensions.
All inputs are finite; a program needn't handle non-finite values.
Results may differ from the reference program's by a relative error of at most 0.0003.
Values sent between devices are 32-bit elements; how exact they have to be, the bound alone decides.
No kernel may reach another device: no remote copies, remote signals or barrier semaphores. Data moves between devices by JAX's collectives and lax.ppermute only.
A program may use at most 256 MiB of HBM per device.

```python
import math
import jax
import jax.numpy as jnp
from jax import lax

P_SIZE = 1024
ITERS = 2
BLK_DEV = 2
BLOCKS = 32
N_FSDP = 16


def row_scales(key, lowest, highest):
    uniform_part = jax.random.uniform(jax.random.fold_in(key, 101), (BLOCKS, P_SIZE), jnp.float32)
    return jnp.exp(math.log(lowest) + uniform_part * (math.log(highest) - math.log(lowest)))


def draw_statistics(key, part):
    scales = row_scales(key, 0.5, 2.0)
    key = jax.random.fold_in(key, 1)
    full_shape = (BLOCKS, P_SIZE, P_SIZE)
    entries = jax.random.normal(key, full_shape, jnp.float32)
    noise = (entries + jnp.swapaxes(entries, 1, 2)) * (0.7071068 * 0.3 / math.sqrt(P_SIZE))
    half_scales = jnp.sqrt(scales)
    identity = jnp.eye(P_SIZE, dtype=jnp.float32)
    return half_scales[:, :, None] * half_scales[:, None, :] * (identity + noise)


def draw_warm_roots(key, part):
    scales = row_scales(key, 0.5, 2.0)
    key = jax.random.fold_in(key, 2)
    full_shape = (BLOCKS, P_SIZE, P_SIZE)
    entries = jax.random.normal(key, full_shape, jnp.float32)
    noise = entries * (0.25 / math.sqrt(P_SIZE))
    eighth_scales = jnp.exp(-0.125 * jnp.log(scales))
    identity = jnp.eye(P_SIZE, dtype=jnp.float32)
    return eighth_scales[:, :, None] * eighth_scales[:, None, :] * (identity + noise)


def draw_orders(key, part):
    key = jax.random.fold_in(key, 3)
    drawn = jax.random.randint(jax.random.fold_in(key, 202), (BLOCKS,), 0, 5)
    picks = jax.random.permutation(jax.random.fold_in(key, 203), BLOCKS)
    drawn = drawn.at[picks[0]].set(4)
    drawn = drawn.at[picks[1]].set(0)
    return (P_SIZE // 2 + drawn * (P_SIZE // 8)).astype(jnp.int32)


def setup_inputs(seed: int = 0) -> dict:
    seeds = jax.random.split(jax.random.key(seed), 4)
    return {
        "statistics": draw_statistics(jax.random.fold_in(seeds[3], 71), 0),
        "warm_roots": draw_warm_roots(jax.random.fold_in(seeds[3], 71), 0),
        "orders": draw_orders(jax.random.fold_in(seeds[3], 71), 0),
    }


def matmul(first_matrix, second_matrix):
    return jnp.dot(first_matrix, second_matrix, precision=lax.Precision.HIGHEST, preferred_element_type=jnp.float32)


def live_root(statistic, warm_root, live_order):
    identity = jnp.eye(live_order, dtype=jnp.float32)
    root = warm_root[:live_order, :live_order]
    square = matmul(root, root)
    fourth = matmul(square, square)
    moment = matmul(fourth, statistic[:live_order, :live_order])
    for sweep in range(ITERS):
        factor = (5.0 * identity - moment) * 0.25
        root = matmul(root, factor)
        if sweep + 1 < ITERS:
            square = matmul(factor, factor)
            moment = matmul(matmul(square, square), moment)
    return jnp.pad(root, ((0, P_SIZE - live_order), (0, P_SIZE - live_order)))


def make_branch(live_order):
    def branch(statistic, warm_root):
        return live_root(statistic, warm_root, live_order)
    return branch


def dealt_places(orders):
    indices = jnp.arange(BLOCKS, dtype=jnp.int32)
    levels = ((orders - P_SIZE // 2) // (P_SIZE // 8)).astype(jnp.int32)
    scores = levels * BLOCKS + indices
    ranked = jnp.argsort(-scores).astype(jnp.int32)
    position = jnp.zeros((BLOCKS,), jnp.int32).at[ranked].set(indices)
    round_ids = position // N_FSDP
    within = position % N_FSDP
    owner_ids = jnp.where(round_ids % 2 == 0, within, N_FSDP - 1 - within)
    return (owner_ids * BLK_DEV + round_ids).astype(jnp.int32)


def reference(statistics, warm_roots, orders):
    branches = [make_branch(P_SIZE // 2 + level * (P_SIZE // 8)) for level in range(5)]

    def one_block(inputs):
        statistic, warm_root, live_order = inputs
        level = ((live_order - P_SIZE // 2) // (P_SIZE // 8)).astype(jnp.int32)
        return lax.switch(level, branches, statistic, warm_root)

    computed = lax.map(one_block, (statistics, warm_roots, orders))
    places = dealt_places(orders)
    return jnp.zeros_like(computed).at[places].set(computed)
```

```python
import functools

import jax
import jax.numpy as jnp
import numpy as np
from jax import lax
from jax.experimental import pallas as pl
from jax.experimental.pallas import tpu as pltpu
from jax.sharding import Mesh
from jax.sharding import PartitionSpec as P

CLASSES = 5
SUBS = 16
LANES = 128
F_ROOT = 0.2720217172
F_CONST = 0.8666936427
G_CONST = 1.4422628010
G_LIN = -0.4526706801
G_SQ = -1.5220217172
LEVELS = ((156, 40), (184, 47), (208, 47), (232, 56), (284, 56))


def chunk_rows(tiles, chunk):
    first = (tiles + 1) // 2 if tiles != 7 else 3
    return (0, first) if chunk == 0 else (first, tiles - first)


def strip_units(tiles, chunk, layers):
    count = chunk_rows(tiles, chunk)[1]
    return -(-count // layers) * tiles


def unit_table(chunk, layers):
    return [strip_units(4 + level, chunk, layers) for level in range(CLASSES)]


def lanes(start, units):
    return pl.ds(pl.multiple_of(start * LANES, LANES), units * LANES)


def any_spec():
    return pl.BlockSpec(memory_space=pl.ANY)


def vmem_spec():
    return pl.BlockSpec(memory_space=pltpu.VMEM)


def smem_spec():
    return pl.BlockSpec(memory_space=pltpu.SMEM)


def for_class(tiles, body):
    for level in range(CLASSES):
        pl.when(tiles == 4 + level)(functools.partial(body, 4 + level))


def split(value):
    high = value.astype(jnp.bfloat16)
    return high, (value - high.astype(jnp.float32)).astype(jnp.bfloat16)


def new_root(statistics, warm_roots, tiles, core, layers):
    size = statistics.shape[1]
    tile = size // 8
    cols = 2 * tile
    out_shapes = [
        jax.ShapeDtypeStruct((SUBS * layers, 8, strip_units(8, chunk, layers) * LANES), jnp.float32)
        for chunk in range(2)
    ]

    def kernel(tiles_ref, core_ref, stat_ref, warm_ref, out0, out1, *scratch):
        full0, full1, warm, stat, first, second, third, load_sems, store_sems = scratch
        outs = (out0, out1)
        order = tiles_ref[0] * tile

        load_warm = pltpu.make_async_copy(warm_ref.at[core_ref[0]], full0, load_sems.at[0])
        load_stat = pltpu.make_async_copy(stat_ref.at[core_ref[0]], full1, load_sems.at[1])
        load_warm.start()
        load_stat.start()

        def place_at(at):
            shape = (size, cols)
            return (
                lax.broadcasted_iota(jnp.int32, shape, 0),
                lax.broadcasted_iota(jnp.int32, shape, 1) + at,
            )

        def identity(at):
            row_ids, col_ids = place_at(at)
            return (row_ids == col_ids) & (col_ids < order)

        def each(body):
            def step(index, _):
                at = pl.multiple_of(index * cols, cols)
                body(at, pl.ds(at, cols))

            lax.fori_loop(0, size // cols, step, None)

        def keep(pair, view, value):
            high, low = split(value)
            pair[0, :, view] = high
            pair[1, :, view] = low

        def take_live(source, pair):
            def body(at, view):
                row_ids, col_ids = place_at(at)
                keep(pair, view, jnp.where((row_ids < order) & (col_ids < order), source[:, view], 0.0))

            each(body)

        def dot(left, right, view):
            def part(i, j):
                return jnp.dot(left[i], right[j, :, view], preferred_element_type=jnp.float32)

            return part(0, 0) + part(0, 1) + part(1, 0)

        load_warm.wait()
        take_live(full0, warm)
        each(lambda at, view: keep(first, view, dot(warm, warm, view)))
        each(lambda at, view: keep(second, view, dot(first, first, view)))
        load_stat.wait()
        take_live(full1, stat)

        def make_factor(at, view):
            moment = dot(second, stat, view)
            value = (jnp.where(identity(at), 5.0, 0.0) - moment) * 0.25
            full0[:, view] = value
            keep(first, view, value)

        each(make_factor)

        def make_square(at, view):
            value = dot(first, first, view)
            full1[:, view] = value
            keep(third, view, value)

        each(make_square)

        def make_polynomials(at, view):
            cube = dot(third, first, view)
            factor, square = (full0[:, view], full1[:, view])
            keep(second, view, cube + F_ROOT * square + F_CONST * factor)
            diagonal = jnp.where(identity(at), G_CONST, 0.0)
            keep(stat, view, cube + G_SQ * square + G_LIN * factor + diagonal)

        each(make_polynomials)
        each(lambda at, view: keep(first, view, dot(warm, second, view)))

        def make_root(at, view):
            full0[:, view] = dot(first, stat, view)

        each(make_root)
        tiled = full0.reshape(8, SUBS, 8, size)

        def copies(count):
            made = []
            for chunk in range(2):
                begin, rows = chunk_rows(count, chunk)
                for row in range(rows):
                    made.append(
                        pltpu.make_async_copy(
                            tiled.at[begin + row, :, :, pl.ds(0, count * LANES)],
                            outs[chunk].at[
                                pl.ds((row % layers) * SUBS, SUBS),
                                :,
                                pl.ds((row // layers) * count * LANES, count * LANES),
                            ],
                            store_sems.at[begin + row],
                        )
                    )
            return made

        def store(count):
            for copy in copies(count):
                copy.start()
            for copy in copies(count):
                copy.wait()

        for_class(tiles_ref[0], store)

    pair = pltpu.VMEM((2, size, size), jnp.bfloat16)
    return pl.pallas_call(
        kernel,
        out_shape=out_shapes,
        in_specs=[smem_spec()] * 2 + [any_spec()] * 2,
        out_specs=[any_spec()] * 2,
        scratch_shapes=[pltpu.VMEM((size, size), jnp.float32)] * 2
        + [pair] * 5
        + [pltpu.SemaphoreType.DMA((2,)), pltpu.SemaphoreType.DMA((8,))],
        compiler_params=pltpu.CompilerParams(vmem_limit_bytes=56 * 2**20),
        name="new_root",
    )(tiles, core, statistics, warm_roots)


def pack_cross(spread, tiles, crossing, offsets, chunk, layers, capacity):
    blocks = spread.shape[0]

    def kernel(tiles_ref, crossing_ref, offsets_ref, spread_ref, out_ref, sems):
        def copy(block, count):
            units = strip_units(count, chunk, layers)
            return pltpu.make_async_copy(
                spread_ref.at[block, :, pl.ds(0, units * LANES)],
                out_ref.at[:, lanes(offsets_ref[block], units)],
                sems.at[block],
            )

        def start(block, _):
            @pl.when(crossing_ref[block] == 1)
            def _():
                for_class(tiles_ref[block], lambda count: copy(block, count).start())

        def wait(block, _):
            @pl.when(crossing_ref[block] == 1)
            def _():
                for_class(tiles_ref[block], lambda count: copy(block, count).wait())

        lax.fori_loop(0, blocks, start, None)
        lax.fori_loop(0, blocks, wait, None)

    return pl.pallas_call(
        kernel,
        out_shape=jax.ShapeDtypeStruct((8, capacity * LANES), jnp.float32),
        in_specs=[smem_spec()] * 3 + [vmem_spec()],
        out_specs=any_spec(),
        scratch_shapes=[pltpu.SemaphoreType.DMA((blocks,))],
        name=f"pack_cross_{chunk}",
    )(tiles, crossing, offsets, spread)


def pack_deliver(spread, crossed, tiles, far, source, target, chunk, layers, capacity):
    places = spread.shape[0]

    def kernel(tiles_ref, far_ref, source_ref, target_ref, spread_ref, crossed_ref, out_ref, sems):
        def copy(place, count, from_far):
            units = strip_units(count, chunk, layers)
            if from_far:
                origin = crossed_ref.at[:, lanes(source_ref[place], units)]
            else:
                origin = spread_ref.at[source_ref[place], :, pl.ds(0, units * LANES)]
            return pltpu.make_async_copy(
                origin, out_ref.at[place // 2, :, lanes(target_ref[place], units)], sems.at[place]
            )

        def each(place, act):
            @pl.when(far_ref[place] == 1)
            def _():
                for_class(tiles_ref[place], lambda count: act(copy(place, count, True)))

            @pl.when(far_ref[place] == 0)
            def _():
                for_class(tiles_ref[place], lambda count: act(copy(place, count, False)))

        lax.fori_loop(0, places, lambda place, _: each(place, lambda c: c.start()), None)
        lax.fori_loop(0, places, lambda place, _: each(place, lambda c: c.wait()), None)

    return pl.pallas_call(
        kernel,
        out_shape=jax.ShapeDtypeStruct((places // 2, 8, capacity * LANES), jnp.float32),
        in_specs=[smem_spec()] * 4 + [vmem_spec()] * 2,
        out_specs=any_spec(),
        scratch_shapes=[pltpu.SemaphoreType.DMA((places,))],
        name=f"pack_deliver_{chunk}",
    )(tiles, far, source, target, spread, crossed)


def assemble(own, other, tiles, core, layers):
    per_layer = SUBS // 2

    def kernel(tiles_ref, core_ref, own0, own1, other0, other1, out_ref, zeros, sems, fill_sems):
        zeros[...] = jnp.zeros_like(zeros)
        sources = ((own0, own1), (other0, other1))

        def copies(block, count):
            made = []
            for chunk in range(2):
                first, rows = chunk_rows(count, chunk)
                for row in range(rows):
                    if block == 0:
                        base = 0
                    else:
                        table = unit_table(chunk, layers)
                        base = sum(
                            jnp.where(tiles_ref[0] == 4 + level, table[level], 0)
                            for level in range(CLASSES)
                        )
                    start = base + (row // layers) * count
                    layer = row % layers
                    for side in range(2):
                        which = core_ref[0] if side == 0 else 1 - core_ref[0]
                        made.append(
                            pltpu.make_async_copy(
                                sources[side][chunk].at[
                                    pl.ds(layer * per_layer, per_layer), :, lanes(start, count)
                                ],
                                out_ref.at[block, first + row, :, which, :, pl.ds(0, count * LANES)],
                                sems.at[block, side, first + row],
                            )
                        )
            return made

        def fills(block, count):
            made = []
            for row in range(8):
                begin = count * LANES if row < count else 0
                if begin == 8 * LANES:
                    continue
                made.append(
                    pltpu.make_async_copy(
                        zeros.at[:, :, :, pl.ds(begin, 8 * LANES - begin)],
                        out_ref.at[block, row, :, :, :, pl.ds(begin, 8 * LANES - begin)],
                        fill_sems.at[block, row],
                    )
                )
            return made

        for block in range(2):

            def start(count, block=block):
                for copy in copies(block, count) + fills(block, count):
                    copy.start()

            for_class(tiles_ref[block], start)
        for block in range(2):

            def wait(count, block=block):
                for copy in copies(block, count) + fills(block, count):
                    copy.wait()

            for_class(tiles_ref[block], wait)

    shape = (2, 8, per_layer, 2, 8, 8 * LANES)
    return pl.pallas_call(
        kernel,
        out_shape=jax.ShapeDtypeStruct(shape, jnp.float32),
        in_specs=[smem_spec()] * 2 + [vmem_spec()] * 4,
        out_specs=any_spec(),
        scratch_shapes=[
            pltpu.VMEM(shape[2:], jnp.float32),
            pltpu.SemaphoreType.DMA((2, 2, 8)),
            pltpu.SemaphoreType.DMA((2, 8)),
        ],
        name="assemble",
    )(tiles, core, *own, *other)


def on_device(statistics, warm_roots, orders):
    blocks, order_pad = (statistics.shape[0], statistics.shape[1])
    quads = lax.axis_size("quad")
    owners = 2 * quads
    all_blocks = orders.shape[0]
    half_blocks = all_blocks // 2
    layers = owners // SUBS
    half = lax.axis_index("half")
    quad = lax.axis_index("quad")
    core = lax.axis_index("rep")
    home = half * quads + quad
    tile = order_pad // 8

    tiles = orders // tile
    indices = jnp.arange(all_blocks, dtype=jnp.int32)
    scores = tiles * all_blocks + indices
    rank = jnp.sum((scores[None, :] > scores[:, None]).astype(jnp.int32), axis=1)
    round_ids = rank // owners
    within = rank % owners
    owner_ids = jnp.where(round_ids % 2 == 0, within, owners - 1 - within)
    target = owner_ids * blocks + round_ids
    hit = (target[None, :] == indices[:, None]).astype(jnp.int32)
    source_of = jnp.sum(hit * indices[None, :], axis=1)
    place_tiles = jnp.sum(hit * tiles[None, :], axis=1)
    block_half = indices // half_blocks
    crossing = (owner_ids // quads != block_half).astype(jnp.int32)
    before = (indices[None, :] < indices[:, None]) & (block_half[None, :] == block_half[:, None])
    before = before.astype(jnp.int32)
    source_half = source_of // half_blocks
    far = (source_half != block_half).astype(jnp.int32)

    def mine(vector):
        return lax.dynamic_slice_in_dim(vector, half * half_blocks, half_blocks, 0)

    plans = []
    needs = []
    for chunk in range(2):
        table = unit_table(chunk, layers)
        units = sum(jnp.where(tiles == 4 + level, table[level], 0) for level in range(CLASSES))
        place_units = jnp.sum(hit * units[None, :], axis=1)
        cross_at = jnp.sum(before * (crossing * units)[None, :], axis=1)
        cross_need = jnp.max(cross_at + crossing * units)
        pair = place_units.reshape(owners, blocks)
        deliver_need = jnp.max(jnp.sum(pair, axis=1))
        origin = jnp.where(
            far == 1, jnp.sum(hit * cross_at[None, :], axis=1), source_of % half_blocks
        )
        to_at = jnp.stack([jnp.zeros((owners,), jnp.int32), pair[:, 0]], axis=1).reshape(-1)
        plans.append((mine(cross_at), mine(origin), mine(to_at)))
        needs.append((cross_need, deliver_need))
    my_tiles, my_crossing = (mine(tiles), mine(crossing))
    my_place_tiles, my_far = (mine(place_tiles), mine(far))
    out_tiles = lax.dynamic_slice_in_dim(place_tiles, home * blocks, blocks, 0)
    own_tiles = lax.dynamic_slice_in_dim(tiles, home * blocks + core, 1, 0)

    core_id = jnp.reshape(core, (1,)).astype(jnp.int32)
    strips0, strips1 = new_root(statistics, warm_roots, own_tiles, core_id, layers)

    group = ("quad", "rep")

    def to_group(strips):
        return lax.all_to_all(strips, group, split_axis=0, concat_axis=0, tiled=True)

    spread0 = to_group(strips0)

    full_cross = [half_blocks * unit_table(chunk, layers)[-1] for chunk in range(2)]
    full_deliver = [2 * unit_table(chunk, layers)[-1] for chunk in range(2)]
    base_cross, base_deliver = (512, 64)
    levels = [
        (
            [-(-cross * full // base_cross) for full in full_cross],
            [-(-deliver * full // base_deliver) for full in full_deliver],
        )
        for cross, deliver in LEVELS
    ]
    levels.append((full_cross, full_deliver))

    def make_route(cross_caps, deliver_caps):
        def route(spread0, strips1):
            def cross(chunk, spread):
                packed = pack_cross(
                    spread, my_tiles, my_crossing, plans[chunk][0], chunk, layers, cross_caps[chunk]
                )
                return lax.ppermute(packed, "half", [(0, 1), (1, 0)])

            def deliver(chunk, spread, crossed):
                packed = pack_deliver(
                    spread,
                    crossed,
                    my_place_tiles,
                    my_far,
                    plans[chunk][1],
                    plans[chunk][2],
                    chunk,
                    layers,
                    deliver_caps[chunk],
                )
                own = lax.all_to_all(packed, "quad", split_axis=0, concat_axis=0, tiled=True)
                return own, lax.ppermute(own, "rep", [(0, 1), (1, 0)])

            crossed0 = cross(0, spread0)
            spread1 = to_group(strips1)
            crossed1 = cross(1, spread1)
            own0, other0 = deliver(0, spread0, crossed0)
            own1, other1 = deliver(1, spread1, crossed1)
            return assemble((own0, own1), (other0, other1), out_tiles, core_id, layers)

        return route

    level = jnp.int32(0)
    for cross_caps, deliver_caps in levels[:-1]:
        fits = jnp.bool_(True)
        for chunk in range(2):
            fits = fits & (needs[chunk][0] <= cross_caps[chunk])
            fits = fits & (needs[chunk][1] <= deliver_caps[chunk])
        level = level + jnp.where(fits, 0, 1)
    result = lax.switch(level, [make_route(*caps) for caps in levels], spread0, strips1)
    return result.reshape(blocks, order_pad, order_pad)


def solution(mesh):
    owners, replicas = (mesh.shape["fsdp"], mesh.shape["rep"])
    devices = np.asarray(mesh.devices).reshape(2, owners // 2, replicas)
    halves = Mesh(devices, ("half", "quad", "rep"))
    whole = P(("half", "quad"), None, None)
    return jax.shard_map(
        on_device, mesh=halves, in_specs=(whole, whole, P()), out_specs=whole, check_vma=False
    )
```

```python
import functools
import math

import jax
import jax.numpy as jnp
import numpy as np
from jax import lax
from jax.experimental import pallas as pl
from jax.experimental.pallas import tpu as pltpu
from jax.sharding import Mesh
from jax.sharding import PartitionSpec as P

CLASSES = 5
SUBS = 16
LANES = 128
ROW_BAND, COL_BAND = (512, 1024)
F_ROOT = 0.2720217172
F_CONST = 0.8666936427
G_CONST = 1.4422628010
G_LIN = -0.4526706801
G_SQ = -1.5220217172
FIRST_ROWS = {4: 2, 5: 3, 6: 3, 7: 3, 8: 4}
LEVELS = (
    ((160, 172), (40, 40)),
    ((175, 188), (47, 47)),
    ((205, 219), (47, 47)),
    ((240, 256), (56, 56)),
    ((290, 305), (56, 56)),
)


def chunk_rows(tiles, chunk):
    first = FIRST_ROWS[tiles]
    return (0, first) if chunk == 0 else (first, tiles - first)


def strip_units(tiles, chunk, layers):
    count = chunk_rows(tiles, chunk)[1]
    return -(-count // layers) * tiles


def unit_table(chunk, layers):
    return [strip_units(4 + level, chunk, layers) for level in range(CLASSES)]


def lanes(start, units):
    return pl.ds(pl.multiple_of(start * LANES, LANES), units * LANES)


def any_spec():
    return pl.BlockSpec(memory_space=pl.ANY)


def vmem_spec():
    return pl.BlockSpec(memory_space=pltpu.VMEM)


def smem_spec():
    return pl.BlockSpec(memory_space=pltpu.SMEM)


SCHEDULE_FLOPS = 3 * 10**10


def cost(moved, flops=0):
    return pl.CostEstimate(flops=flops, bytes_accessed=moved, transcendentals=0)


def loop(first, stop, body):
    lax.fori_loop(first, stop, lambda index, _: body(index), None)


def both_passes(run):
    run(lambda copy: copy.start())
    run(lambda copy: copy.wait())


def for_class(tiles, body):
    for level in range(CLASSES):
        pl.when(tiles == 4 + level)(functools.partial(body, 4 + level))


def split(value):
    high = value.astype(jnp.bfloat16)
    return high, (value - high.astype(jnp.float32)).astype(jnp.bfloat16)


def new_root(statistics, warm_roots, orders, ids, layers):
    size = statistics.shape[1]
    tile = size // 8
    def kernel(ids_ref, orders_ref, stat_ref, warm_ref, out0, out1, *scratch):
        full0, full1, warm, stat, first, second, third, load_sems, store_sems = scratch
        core = ids_ref[0]
        order = orders_ref[ids_ref[2]]
        tiles = order // tile

        def load(source, target, which):
            return [
                pltpu.make_async_copy(
                    source.at[core, pl.ds(row * tile, tile), :],
                    target.at[pl.ds(row * tile, tile), :],
                    load_sems.at[which, row],
                )
                for row in range(8)
            ]

        load_warm = load(warm_ref, full0, 0)
        load_stat = load(stat_ref, full1, 1)
        for copy in load_warm:
            copy.start()

        def keep(pair, rows, view, value):
            high, low = split(value)
            pair[0, rows, view] = high
            pair[1, rows, view] = low

        live_cols = jnp.where(lax.broadcasted_iota(jnp.int32, (1, size), 1) < order, 1.0, 0.0)

        every = slice(0, size)

        def live_rows(rows):
            row_ids = lax.broadcasted_iota(jnp.int32, (rows.size, 1), 0) + rows.start
            return jnp.where(row_ids < order, 1.0, 0.0)

        def take_live(source, pair, row):
            rows = pl.ds(row * tile, tile)
            live = live_cols * jnp.where(row < tiles, 1.0, 0.0)
            keep(pair, rows, slice(0, size), source[rows, :] * live)

        def dot(left, right, rows, view):
            def part(i, j):
                return jnp.dot(left[i, rows, :], right[j, :, view], preferred_element_type=jnp.float32)

            return part(0, 0) + part(0, 1) + part(1, 0)

        def each(body):
            def step(index, _):
                rows = pl.ds(pl.multiple_of(index * ROW_BAND, ROW_BAND), ROW_BAND)
                for at in range(0, size, COL_BAND):
                    body(rows, slice(at, at + COL_BAND))

            lax.fori_loop(0, size // ROW_BAND, step, None)

        def add_diagonal(source, pair, scale):
            def step(index, _):
                at = pl.multiple_of(index * tile, tile)
                view = pl.ds(at, tile)
                row_ids = lax.broadcasted_iota(jnp.int32, (tile, tile), 0)
                col_ids = lax.broadcasted_iota(jnp.int32, (tile, tile), 1)
                on = (row_ids == col_ids) & (index < tiles)
                value = source[view, view] + jnp.where(on, scale, 0.0)
                source[view, view] = value
                keep(pair, view, view, value)

            lax.fori_loop(0, 8, step, None)

        for row in range(8):
            load_warm[row].wait()
            take_live(full0, warm, row)
        for copy in load_stat:
            copy.start()
        each(lambda rows, view: keep(first, rows, view, dot(warm, warm, rows, view)))
        for copy in load_stat:
            copy.wait()

        def make_fourth(rows, view):
            keep(second, rows, view, dot(first, first, rows, view))
            at = view.start // COL_BAND * (ROW_BAND * COL_BAND // size)
            some = pl.ds(rows.start + at, ROW_BAND * COL_BAND // size)
            live = live_cols * live_rows(some)
            keep(stat, some, every, full1[some, :] * live)

        each(make_fourth)

        def make_factor(rows, view):
            value = dot(second, stat, rows, view) * -0.25
            full0[rows, view] = value
            keep(first, rows, view, value)

        each(make_factor)
        add_diagonal(full0, first, 1.25)

        def make_square(rows, view):
            value = dot(first, first, rows, view)
            full1[rows, view] = value
            keep(third, rows, view, value)

        each(make_square)

        def make_polynomials(rows, view):
            cube = dot(third, first, rows, view)
            factor, square = (full0[rows, view], full1[rows, view])
            keep(second, rows, view, cube + F_ROOT * square + F_CONST * factor)
            value = cube + G_SQ * square + G_LIN * factor
            full1[rows, view] = value
            keep(stat, rows, view, value)

        each(make_polynomials)
        add_diagonal(full1, stat, G_CONST)
        each(lambda rows, view: keep(first, rows, view, dot(warm, second, rows, view)))

        def make_root(rows, view):
            full0[rows, view] = dot(first, stat, rows, view)

        tiled = full0.reshape(8, SUBS, 8, size)

        def copy(chunk, count, row):
            begin = chunk_rows(count, chunk)[0]
            layer = pl.multiple_of(lax.rem(row - begin, layers) * SUBS, SUBS)
            return pltpu.make_async_copy(
                tiled.at[row, :, :, pl.ds(0, count * LANES)],
                (out0, out1)[chunk].at[
                    pl.ds(layer, SUBS), :, lanes((row - begin) // layers * count, count)
                ],
                store_sems.at[row],
            )

        bands = size // ROW_BAND

        def step(index, _):
            rows = pl.ds(pl.multiple_of(index * ROW_BAND, ROW_BAND), ROW_BAND)
            for at in range(0, size, COL_BAND):
                make_root(rows, slice(at, at + COL_BAND))
            first = index * (8 // bands)

            def store(count):
                for chunk in range(2):
                    begin, rows = chunk_rows(count, chunk)
                    loop(
                        jnp.maximum(begin, first),
                        jnp.minimum(begin + rows, first + 8 // bands),
                        lambda row, chunk=chunk: copy(chunk, count, row).start(),
                    )

            for_class(tiles, store)

        lax.fori_loop(0, bands, step, None)

        def wait(count):
            for chunk in range(2):
                begin, rows = chunk_rows(count, chunk)
                loop(begin, begin + rows, lambda row, chunk=chunk: copy(chunk, count, row).wait())

        for_class(tiles, wait)

    pair = pltpu.VMEM((2, size, size), jnp.bfloat16)
    return pl.pallas_call(
        kernel,
        out_shape=[
            jax.ShapeDtypeStruct((SUBS * layers, 8, unit_table(chunk, layers)[-1] * LANES), jnp.float32)
            for chunk in range(2)
        ],
        in_specs=[smem_spec()] * 2 + [any_spec()] * 2,
        out_specs=[any_spec()] * 2,
        scratch_shapes=[pltpu.VMEM((size, size), jnp.float32)] * 2
        + [pair] * 5
        + [pltpu.SemaphoreType.DMA((2, 8)), pltpu.SemaphoreType.DMA((8,))],
        compiler_params=pltpu.CompilerParams(vmem_limit_bytes=56 * 2**20),
        cost_estimate=cost(12 * size * size, 42 * size**3),
        name="new_root",
    )(ids, orders, statistics, warm_roots)


TILES, CROSSING, CROSS_AT, PLACE_TILES, FAR, ORIGIN, TO_AT, PLAN_ROWS = 0, 1, 2, 4, 5, 6, 8, 10


def pack_cross(spread, plan, chunk, layers, capacity):
    blocks = spread.shape[0]

    def kernel(plan_ref, spread_ref, out_ref, sems):
        def copy(block, count):
            units = strip_units(count, chunk, layers)
            start = plan_ref[(CROSS_AT + chunk) * blocks + block]
            return pltpu.make_async_copy(
                spread_ref.at[block, :, pl.ds(0, units * LANES)],
                out_ref.at[:, lanes(start, units)],
                sems.at[block],
            )

        def run(act):
            def each(block):
                @pl.when(plan_ref[CROSSING * blocks + block] == 1)
                def _():
                    tiles = plan_ref[TILES * blocks + block]
                    for_class(tiles, lambda count: act(copy(block, count)))

            loop(0, blocks, each)

        both_passes(run)

    return pl.pallas_call(
        kernel,
        out_shape=jax.ShapeDtypeStruct((8, capacity * LANES), jnp.float32),
        in_specs=[smem_spec(), vmem_spec()],
        out_specs=any_spec(),
        scratch_shapes=[pltpu.SemaphoreType.DMA((blocks,))],
        cost_estimate=cost(4 * spread.size + 32 * capacity * LANES, SCHEDULE_FLOPS),
        name=f"pack_cross_{chunk}",
    )(plan, spread)


def pack_deliver(spread, crossed, plan, chunk, layers, capacity):
    places = spread.shape[0]

    def kernel(plan_ref, spread_ref, crossed_ref, out_ref, sems):
        def copy(place, count, from_far):
            units = strip_units(count, chunk, layers)
            source = plan_ref[(ORIGIN + chunk) * places + place]
            target = plan_ref[(TO_AT + chunk) * places + place]
            if from_far:
                origin = crossed_ref.at[:, lanes(source, units)]
            else:
                origin = spread_ref.at[source, :, pl.ds(0, units * LANES)]
            return pltpu.make_async_copy(
                origin, out_ref.at[place // 2, :, lanes(target, units)], sems.at[place]
            )

        def run(act):
            def each(place):
                for from_far in range(2):

                    @pl.when(plan_ref[FAR * places + place] == from_far)
                    def _(from_far=from_far):
                        tiles = plan_ref[PLACE_TILES * places + place]
                        for_class(tiles, lambda count: act(copy(place, count, from_far == 1)))

            loop(0, places, each)

        both_passes(run)

    return pl.pallas_call(
        kernel,
        out_shape=jax.ShapeDtypeStruct((places // 2, 8, capacity * LANES), jnp.float32),
        in_specs=[smem_spec()] + [vmem_spec()] * 2,
        out_specs=any_spec(),
        scratch_shapes=[pltpu.SemaphoreType.DMA((places,))],
        cost_estimate=cost(4 * (spread.size + crossed.size) + 16 * places * capacity * LANES, SCHEDULE_FLOPS),
        name=f"pack_deliver_{chunk}",
    )(plan, spread, crossed)


def assemble(own, other, plan, ids, chunk, layers, begun=None):
    per_layer = SUBS // 2
    places = plan.shape[0] // PLAN_ROWS
    shape = (2, 8, per_layer, 2, 8, 8 * LANES)

    def kernel(plan_ref, ids_ref, own_ref, other_ref, *rest):
        if chunk == 0:
            out_ref, zeros, sems, fill_sems = rest
            zeros[...] = jnp.zeros_like(zeros)
        else:
            _, out_ref, sems = rest
        core = ids_ref[0]

        def copy(block, count, row, side):
            first = chunk_rows(count, chunk)[0]
            base = plan_ref[(TO_AT + chunk) * places + ids_ref[1] * 2 + block]
            layer = pl.multiple_of(lax.rem(row, layers) * per_layer, per_layer)
            return pltpu.make_async_copy(
                (own_ref, other_ref)[side].at[
                    pl.ds(layer, per_layer), :, lanes(base + row // layers * count, count)
                ],
                out_ref.at[
                    block, first + row, :, core if side == 0 else 1 - core, :, pl.ds(0, count * LANES)
                ],
                sems.at[block, side, row],
            )

        def fill(block, row, begin):
            view = pl.ds(begin * LANES, (8 - begin) * LANES)
            return pltpu.make_async_copy(
                zeros.at[:, :, :, view],
                out_ref.at[block, row, :, :, :, view],
                fill_sems.at[block, row],
            )

        def run(act):
            def each(block):
                def body(count):
                    def one_row(row):
                        act(copy(block, count, row, 0))
                        act(copy(block, count, row, 1))

                    loop(0, chunk_rows(count, chunk)[1], one_row)
                    if chunk == 0 and count < 8:
                        loop(0, count, lambda row: act(fill(block, row, count)))
                        loop(count, 8, lambda row: act(fill(block, row, 0)))

                for_class(plan_ref[PLACE_TILES * places + ids_ref[1] * 2 + block], body)

            loop(0, 2, each)

        both_passes(run)

    scratch = [pltpu.SemaphoreType.DMA((2, 2, 8))]
    if chunk == 0:
        scratch = [pltpu.VMEM(shape[2:], jnp.float32)] + scratch + [pltpu.SemaphoreType.DMA((2, 8))]
    more = [] if begun is None else [begun]
    return pl.pallas_call(
        kernel,
        out_shape=jax.ShapeDtypeStruct(shape, jnp.float32),
        in_specs=[smem_spec()] * 2 + [vmem_spec()] * 2 + [any_spec()] * len(more),
        out_specs=any_spec(),
        scratch_shapes=scratch,
        input_output_aliases={4: 0} if more else {},
        cost_estimate=cost(4 * (own.size + other.size + math.prod(shape) // 2)),
        name=f"assemble_{chunk}",
    )(plan, ids, own, other, *more)


def on_device(statistics, warm_roots, orders):
    blocks, order_pad = (statistics.shape[0], statistics.shape[1])
    quads = lax.axis_size("quad")
    owners = 2 * quads
    all_blocks = orders.shape[0]
    half_blocks = all_blocks // 2
    layers = owners // SUBS
    half = lax.axis_index("half")
    quad = lax.axis_index("quad")
    core = lax.axis_index("rep")
    home = half * quads + quad
    tile = order_pad // 8

    tiles = orders // tile
    indices = jnp.arange(all_blocks, dtype=jnp.int32)
    scores = tiles * all_blocks + indices
    rank = jnp.sum((scores[None, :] > scores[:, None]).astype(jnp.int32), axis=1)
    round_ids = rank // owners
    within = rank % owners
    owner_ids = jnp.where(round_ids % 2 == 0, within, owners - 1 - within)
    target = owner_ids * blocks + round_ids
    hit = (target[None, :] == indices[:, None]).astype(jnp.int32)
    source_of = jnp.sum(hit * indices[None, :], axis=1)
    place_tiles = jnp.sum(hit * tiles[None, :], axis=1)
    block_half = indices // half_blocks
    crossing = (owner_ids // quads != block_half).astype(jnp.int32)
    before = (indices[None, :] < indices[:, None]) & (block_half[None, :] == block_half[:, None])
    before = before.astype(jnp.int32)
    source_half = source_of // half_blocks
    far = (source_half != block_half).astype(jnp.int32)

    cross_ats, origins, to_ats = ([], [], [])
    needs = []
    for chunk in range(2):
        table = unit_table(chunk, layers)
        units = sum(jnp.where(tiles == 4 + level, table[level], 0) for level in range(CLASSES))
        place_units = jnp.sum(hit * units[None, :], axis=1)
        cross_at = jnp.sum(before * (crossing * units)[None, :], axis=1)
        cross_need = jnp.max(cross_at + crossing * units)
        pair = place_units.reshape(owners, blocks)
        deliver_need = jnp.max(jnp.sum(pair, axis=1))
        origin = jnp.where(
            far == 1, jnp.sum(hit * cross_at[None, :], axis=1), source_of % half_blocks
        )
        to_at = jnp.stack([jnp.zeros((owners,), jnp.int32), pair[:, 0]], axis=1).reshape(-1)
        cross_ats.append(cross_at)
        origins.append(origin)
        to_ats.append(to_at)
        needs.append((cross_need, deliver_need))
    plan = jnp.stack([tiles, crossing, *cross_ats, place_tiles, far, *origins, *to_ats])
    plan = lax.dynamic_slice_in_dim(plan, half * half_blocks, half_blocks, 1).reshape(-1)

    ids = jnp.stack([core, quad, home * blocks + core]).astype(jnp.int32)
    strips0, strips1 = new_root(statistics, warm_roots, orders, ids, layers)

    def to_group(strips):
        return lax.all_to_all(strips, ("quad", "rep"), split_axis=0, concat_axis=0, tiled=True)

    spread0 = to_group(strips0)

    fulls = [unit_table(chunk, layers)[-1] for chunk in range(2)]
    one_layer = [unit_table(chunk, 1)[-1] for chunk in range(2)]

    def scaled(units, factor):
        return [-(-units[chunk] * factor * fulls[chunk] // one_layer[chunk]) for chunk in range(2)]

    levels = [
        ([-(-units // SUBS) for units in scaled(cross, half_blocks)], scaled(delivery, 1))
        for cross, delivery in LEVELS
    ]
    levels.append(([half_blocks * full for full in fulls], [2 * full for full in fulls]))

    def make_route(cross_caps, deliver_caps):
        def route(spread0, strips1):
            def swap(array):
                return lax.ppermute(array, "rep", [(0, 1), (1, 0)])

            def across(packed):
                return lax.ppermute(packed, "half", [(0, 1), (1, 0)])

            def deliver(packed):
                return lax.all_to_all(packed, "quad", split_axis=0, concat_axis=0, tiled=True)

            packed0 = pack_cross(spread0, plan, 0, layers, cross_caps[0])
            packed0, strips1 = lax.optimization_barrier((packed0, strips1))
            crossed0 = across(packed0)
            spread1 = to_group(strips1)
            packed1 = pack_cross(spread1, plan, 1, layers, cross_caps[1])
            crossed1 = across(packed1)
            crossed0, _ = lax.optimization_barrier((crossed0, packed1))
            own0 = deliver(pack_deliver(spread0, crossed0, plan, 0, layers, deliver_caps[0]))
            packed1 = pack_deliver(spread1, crossed1, plan, 1, layers, deliver_caps[1])
            own0, packed1 = lax.optimization_barrier((own0, packed1))
            own1 = deliver(packed1)
            begun = assemble(own0, swap(own0), plan, ids, 0, layers)
            own1, begun = lax.optimization_barrier((own1, begun))
            return assemble(own1, swap(own1), plan, ids, 1, layers, begun)

        return route

    level = jnp.int32(0)
    for caps in levels[:-1]:
        short = jnp.bool_(False)
        for chunk in range(2):
            for which in range(2):
                short = short | (needs[chunk][which] > caps[which][chunk])
        level = level + short.astype(jnp.int32)
    routes = [make_route(*caps) for caps in levels]
    result = lax.switch(level, routes, spread0, strips1)
    return result.reshape(blocks, order_pad, order_pad)


def solution(mesh):
    owners, replicas = (mesh.shape["fsdp"], mesh.shape["rep"])
    devices = np.asarray(mesh.devices).reshape(2, owners // 2, replicas)
    halves = Mesh(devices, ("half", "quad", "rep"))
    whole = P(("half", "quad"), None, None)
    return jax.shard_map(
        on_device, mesh=halves, in_specs=(whole, whole, P()), out_specs=whole, check_vma=False
    )
```

```python
import functools
import math

import jax
import jax.numpy as jnp
import numpy as np
from jax import lax
from jax.experimental import pallas as pl
from jax.experimental.pallas import tpu as pltpu
from jax.sharding import Mesh
from jax.sharding import PartitionSpec as P

CLASSES = 5
SUBS = 16
LANES = 128
ROW_BAND, COL_BAND = (512, 1024)
F_ROOT = 0.2720217172
F_CONST = 0.8666936427
G_CONST = 1.4422628010
G_LIN = -0.4526706801
G_SQ = -1.5220217172
FIRST_ROWS = {4: 2, 5: 3, 6: 3, 7: 3, 8: 4}
LEVELS = (
    ((145, 155), (47, 47)),
    ((168, 180), (47, 47)),
    ((190, 204), (47, 47)),
    ((215, 230), (47, 47)),
    ((260, 278), (56, 56)),
)


def chunk_rows(tiles, chunk):
    first = FIRST_ROWS[tiles]
    return (0, first) if chunk == 0 else (first, tiles - first)


def strip_units(tiles, chunk, layers):
    count = chunk_rows(tiles, chunk)[1]
    return -(-count // layers) * tiles


def unit_table(chunk, layers):
    return [strip_units(4 + level, chunk, layers) for level in range(CLASSES)]


def lanes(start, units):
    return pl.ds(pl.multiple_of(start * LANES, LANES), units * LANES)


def any_spec():
    return pl.BlockSpec(memory_space=pl.ANY)


def vmem_spec():
    return pl.BlockSpec(memory_space=pltpu.VMEM)


def smem_spec():
    return pl.BlockSpec(memory_space=pltpu.SMEM)


SCHEDULE_FLOPS = 3 * 10**10


def cost(moved, flops=0):
    return pl.CostEstimate(flops=flops, bytes_accessed=moved, transcendentals=0)


def loop(first, stop, body):
    lax.fori_loop(first, stop, lambda index, _: body(index), None)


def both_passes(run):
    run(lambda copy: copy.start())
    run(lambda copy: copy.wait())


def for_class(tiles, body):
    for level in range(CLASSES):
        pl.when(tiles == 4 + level)(functools.partial(body, 4 + level))


def split(value):
    high = value.astype(jnp.bfloat16)
    return high, (value - high.astype(jnp.float32)).astype(jnp.bfloat16)


def store_rows(source, outs, tiles, span, layers, sems):
    tiled = source.reshape(-1, SUBS, 8, source.shape[1])

    def run(act):
        def store(count):
            for chunk in range(2):
                begin, rows = chunk_rows(count, chunk)

                def one_row(row, begin=begin, chunk=chunk):
                    layer = pl.multiple_of(lax.rem(row - begin, layers) * SUBS, SUBS)
                    act(
                        pltpu.make_async_copy(
                            tiled.at[row - span.start, :, :, pl.ds(0, count * LANES)],
                            outs[chunk].at[
                                pl.ds(layer, SUBS), :, lanes((row - begin) // layers * count, count)
                            ],
                            sems.at[row],
                        )
                    )

                low, high = (max(begin, span.start), min(begin + rows, span.stop))
                if low < high:
                    loop(low, high, one_row)

        for_class(tiles, store)

    both_passes(run)


def split_dot(left, right, rows, view):
    def part(i, j):
        return jnp.dot(left[i, rows, :], right[j, :, view], preferred_element_type=jnp.float32)

    return part(0, 0) + part(0, 1) + part(1, 0)


def new_root(statistics, warm_roots, orders, ids, layers):
    size = statistics.shape[1]
    tile, half = (size // 8, size // 2)

    def kernel(ids_ref, orders_ref, stat_ref, warm_ref, out0, out1, polys_out, warm_out, *scratch):
        full0, full1, warm, stat, first, second, third, load_sems, store_sems, keep_sems = scratch
        core = ids_ref[0]
        order = orders_ref[ids_ref[2]]
        tiles = order // tile

        def load(source, target, which):
            return [
                pltpu.make_async_copy(
                    source.at[core, pl.ds(row * tile, tile), :],
                    target.at[pl.ds(row * tile, tile), :],
                    load_sems.at[which, row],
                )
                for row in range(8)
            ]

        load_warm = load(warm_ref, full0, 0)
        load_stat = load(stat_ref, full1, 1)
        for copy in load_warm:
            copy.start()

        def keep(pair, rows, view, value):
            high, low = split(value)
            pair[0, rows, view] = high
            pair[1, rows, view] = low

        live_cols = jnp.where(lax.broadcasted_iota(jnp.int32, (1, size), 1) < order, 1.0, 0.0)

        every = slice(0, size)

        def live_rows(rows):
            row_ids = lax.broadcasted_iota(jnp.int32, (rows.size, 1), 0) + rows.start
            return jnp.where(row_ids < order, 1.0, 0.0)

        def take_live(source, pair, row):
            rows = pl.ds(row * tile, tile)
            live = live_cols * jnp.where(row < tiles, 1.0, 0.0)
            keep(pair, rows, slice(0, size), source[rows, :] * live)

        def each(body):
            def step(index, _):
                rows = pl.ds(pl.multiple_of(index * ROW_BAND, ROW_BAND), ROW_BAND)
                for at in range(0, size, COL_BAND):
                    body(rows, slice(at, at + COL_BAND))

            lax.fori_loop(0, size // ROW_BAND, step, None)

        def add_diagonal(source, pair, scale):
            def step(index, _):
                at = pl.multiple_of(index * tile, tile)
                view = pl.ds(at, tile)
                row_ids = lax.broadcasted_iota(jnp.int32, (tile, tile), 0)
                col_ids = lax.broadcasted_iota(jnp.int32, (tile, tile), 1)
                on = (row_ids == col_ids) & (index < tiles)
                value = source[view, view] + jnp.where(on, scale, 0.0)
                source[view, view] = value
                keep(pair, view, view, value)

            lax.fori_loop(0, 8, step, None)

        for row in range(8):
            load_warm[row].wait()
            take_live(full0, warm, row)
        for copy in load_stat:
            copy.start()
        each(lambda rows, view: keep(first, rows, view, split_dot(warm, warm, rows, view)))
        for copy in load_stat:
            copy.wait()

        def make_fourth(rows, view):
            keep(second, rows, view, split_dot(first, first, rows, view))
            at = view.start // COL_BAND * (ROW_BAND * COL_BAND // size)
            some = pl.ds(rows.start + at, ROW_BAND * COL_BAND // size)
            live = live_cols * live_rows(some)
            keep(stat, some, every, full1[some, :] * live)

        each(make_fourth)

        def make_factor(rows, view):
            value = split_dot(second, stat, rows, view) * -0.25
            full0[rows, view] = value
            keep(first, rows, view, value)

        each(make_factor)
        add_diagonal(full0, first, 1.25)

        def make_square(rows, view):
            value = split_dot(first, first, rows, view)
            full1[rows, view] = value
            keep(third, rows, view, value)

        each(make_square)

        def make_polynomials(rows, view):
            cube = split_dot(third, first, rows, view)
            factor, square = (full0[rows, view], full1[rows, view])
            keep(second, rows, view, cube + F_ROOT * square + F_CONST * factor)
            value = cube + G_SQ * square + G_LIN * factor
            full1[rows, view] = value
            keep(stat, rows, view, value)

        each(make_polynomials)
        add_diagonal(full1, stat, G_CONST)
        kept = [
            pltpu.make_async_copy(second, polys_out.at[0], keep_sems.at[0]),
            pltpu.make_async_copy(stat, polys_out.at[1], keep_sems.at[1]),
            pltpu.make_async_copy(warm.at[:, pl.ds(half, half), :], warm_out, keep_sems.at[2]),
        ]
        for save in kept:
            save.start()
        upper = slice(0, half)
        keep(first, upper, every, split_dot(warm, second, upper, every))
        full0[upper, :] = split_dot(first, stat, upper, every)
        store_rows(full0, (out0, out1), tiles, range(0, 4), layers, store_sems)
        for save in kept:
            save.wait()

    pair = pltpu.VMEM((2, size, size), jnp.bfloat16)
    return pl.pallas_call(
        kernel,
        out_shape=[
            jax.ShapeDtypeStruct((SUBS * layers, 8, unit_table(chunk, layers)[-1] * LANES), jnp.float32)
            for chunk in range(2)
        ]
        + [
            jax.ShapeDtypeStruct((2, 2, size, size), jnp.bfloat16),
            jax.ShapeDtypeStruct((2, half, size), jnp.bfloat16),
        ],
        in_specs=[smem_spec()] * 2 + [any_spec()] * 2,
        out_specs=[any_spec()] * 4,
        scratch_shapes=[pltpu.VMEM((size, size), jnp.float32)] * 2
        + [pair] * 5
        + [pltpu.SemaphoreType.DMA((2, 8)), pltpu.SemaphoreType.DMA((8,)), pltpu.SemaphoreType.DMA((3,))],
        compiler_params=pltpu.CompilerParams(vmem_limit_bytes=56 * 2**20),
        cost_estimate=cost(20 * size * size, 36 * size**3),
        name="new_root",
    )(ids, orders, statistics, warm_roots)


def rest_of_root(strips, polys, warm, orders, ids, layers):
    half, size = warm.shape[1:]

    def kernel(ids_ref, orders_ref, _, polys_ref, warm_ref, out_ref, *scratch):
        poly, left, right, product, load_sems, store_sems = scratch
        loads = [
            pltpu.make_async_copy(warm_ref, left, load_sems.at[0]),
            pltpu.make_async_copy(polys_ref.at[0], poly.at[0], load_sems.at[1]),
            pltpu.make_async_copy(polys_ref.at[1], poly.at[1], load_sems.at[2]),
        ]
        for load in loads:
            load.start()
        every = slice(0, size)
        rows = slice(0, half)
        loads[0].wait()
        loads[1].wait()
        high, low = split(split_dot(left, poly.at[0], rows, every))
        right[0] = high
        right[1] = low
        loads[2].wait()
        product[...] = split_dot(right, poly.at[1], rows, every)
        tiles = orders_ref[ids_ref[2]] // (size // 8)
        store_rows(product, (None, out_ref), tiles, range(4, 8), layers, store_sems)

    part = pltpu.VMEM((2, half, size), jnp.bfloat16)
    return pl.pallas_call(
        kernel,
        out_shape=jax.ShapeDtypeStruct(strips.shape, strips.dtype),
        in_specs=[smem_spec()] * 2 + [any_spec()] * 3,
        out_specs=any_spec(),
        scratch_shapes=[pltpu.VMEM((2, 2, size, size), jnp.bfloat16), part, part]
        + [pltpu.VMEM((half, size), jnp.float32)]
        + [pltpu.SemaphoreType.DMA((3,)), pltpu.SemaphoreType.DMA((8,))],
        input_output_aliases={2: 0},
        compiler_params=pltpu.CompilerParams(vmem_limit_bytes=40 * 2**20),
        cost_estimate=cost(12 * size * size, 6 * size**3),
        name="rest_of_root",
    )(ids, orders, strips, polys, warm)


TILES, CROSSING, CROSS_AT, PLACE_TILES, FAR, ORIGIN, TO_AT, PLAN_ROWS = 0, 1, 2, 4, 5, 6, 8, 10


def pack_cross(spread, plan, chunk, layers, capacity):
    blocks = spread.shape[0]

    def kernel(plan_ref, spread_ref, out_ref, sems):
        def copy(block, count):
            units = strip_units(count, chunk, layers)
            start = plan_ref[(CROSS_AT + chunk) * blocks + block]
            return pltpu.make_async_copy(
                spread_ref.at[block, :, pl.ds(0, units * LANES)],
                out_ref.at[:, lanes(start, units)],
                sems.at[block],
            )

        def run(act):
            def each(block):
                @pl.when(plan_ref[CROSSING * blocks + block] == 1)
                def _():
                    tiles = plan_ref[TILES * blocks + block]
                    for_class(tiles, lambda count: act(copy(block, count)))

            loop(0, blocks, each)

        both_passes(run)

    return pl.pallas_call(
        kernel,
        out_shape=jax.ShapeDtypeStruct((8, capacity * LANES), jnp.float32),
        in_specs=[smem_spec(), vmem_spec()],
        out_specs=any_spec(),
        scratch_shapes=[pltpu.SemaphoreType.DMA((blocks,))],
        cost_estimate=cost(4 * spread.size + 32 * capacity * LANES, SCHEDULE_FLOPS),
        name=f"pack_cross_{chunk}",
    )(plan, spread)


def pack_deliver(spread, crossed, plan, chunk, layers, capacity):
    places = spread.shape[0]

    def kernel(plan_ref, spread_ref, crossed_ref, out_ref, sems):
        def copy(place, count, from_far):
            units = strip_units(count, chunk, layers)
            source = plan_ref[(ORIGIN + chunk) * places + place]
            target = plan_ref[(TO_AT + chunk) * places + place]
            if from_far:
                origin = crossed_ref.at[:, lanes(source, units)]
            else:
                origin = spread_ref.at[source, :, pl.ds(0, units * LANES)]
            return pltpu.make_async_copy(
                origin, out_ref.at[place // 2, :, lanes(target, units)], sems.at[place]
            )

        def run(act):
            def each(place):
                for from_far in range(2):

                    @pl.when(plan_ref[FAR * places + place] == from_far)
                    def _(from_far=from_far):
                        tiles = plan_ref[PLACE_TILES * places + place]
                        for_class(tiles, lambda count: act(copy(place, count, from_far == 1)))

            loop(0, places, each)

        both_passes(run)

    return pl.pallas_call(
        kernel,
        out_shape=jax.ShapeDtypeStruct((places // 2, 8, capacity * LANES), jnp.float32),
        in_specs=[smem_spec()] + [vmem_spec()] * 2,
        out_specs=any_spec(),
        scratch_shapes=[pltpu.SemaphoreType.DMA((places,))],
        cost_estimate=cost(4 * (spread.size + crossed.size) + 16 * places * capacity * LANES, SCHEDULE_FLOPS),
        name=f"pack_deliver_{chunk}",
    )(plan, spread, crossed)


def assemble(own, other, plan, ids, chunk, layers, begun=None):
    per_layer = SUBS // 2
    places = plan.shape[0] // PLAN_ROWS
    shape = (2, 8, per_layer, 2, 8, 8 * LANES)

    def kernel(plan_ref, ids_ref, own_ref, other_ref, *rest):
        if chunk == 0:
            out_ref, zeros, sems, fill_sems = rest
            zeros[...] = jnp.zeros_like(zeros)
        else:
            _, out_ref, sems = rest
        core = ids_ref[0]

        def copy(block, count, row, side):
            first = chunk_rows(count, chunk)[0]
            base = plan_ref[(TO_AT + chunk) * places + ids_ref[1] * 2 + block]
            layer = pl.multiple_of(lax.rem(row, layers) * per_layer, per_layer)
            return pltpu.make_async_copy(
                (own_ref, other_ref)[side].at[
                    pl.ds(layer, per_layer), :, lanes(base + row // layers * count, count)
                ],
                out_ref.at[
                    block, first + row, :, core if side == 0 else 1 - core, :, pl.ds(0, count * LANES)
                ],
                sems.at[block, side, row],
            )

        def fill(block, row, begin):
            view = pl.ds(begin * LANES, (8 - begin) * LANES)
            return pltpu.make_async_copy(
                zeros.at[:, :, :, view],
                out_ref.at[block, row, :, :, :, view],
                fill_sems.at[block, row],
            )

        def run(act):
            def each(block):
                def body(count):
                    def one_row(row):
                        act(copy(block, count, row, 0))
                        act(copy(block, count, row, 1))

                    loop(0, chunk_rows(count, chunk)[1], one_row)
                    if chunk == 0 and count < 8:
                        loop(0, count, lambda row: act(fill(block, row, count)))
                        loop(count, 8, lambda row: act(fill(block, row, 0)))

                for_class(plan_ref[PLACE_TILES * places + ids_ref[1] * 2 + block], body)

            loop(0, 2, each)

        both_passes(run)

    scratch = [pltpu.SemaphoreType.DMA((2, 2, 8))]
    if chunk == 0:
        scratch = [pltpu.VMEM(shape[2:], jnp.float32)] + scratch + [pltpu.SemaphoreType.DMA((2, 8))]
    more = [] if begun is None else [begun]
    return pl.pallas_call(
        kernel,
        out_shape=jax.ShapeDtypeStruct(shape, jnp.float32),
        in_specs=[smem_spec()] * 2 + [vmem_spec()] * 2 + [any_spec()] * len(more),
        out_specs=any_spec(),
        scratch_shapes=scratch,
        input_output_aliases={4: 0} if more else {},
        cost_estimate=cost(4 * (own.size + other.size + math.prod(shape) // 2)),
        name=f"assemble_{chunk}",
    )(plan, ids, own, other, *more)


def on_device(statistics, warm_roots, orders):
    blocks, order_pad = (statistics.shape[0], statistics.shape[1])
    quads = lax.axis_size("quad")
    owners = 2 * quads
    all_blocks = orders.shape[0]
    half_blocks = all_blocks // 2
    layers = owners // SUBS
    half = lax.axis_index("half")
    quad = lax.axis_index("quad")
    core = lax.axis_index("rep")
    home = half * quads + quad
    tile = order_pad // 8

    tiles = orders // tile
    indices = jnp.arange(all_blocks, dtype=jnp.int32)
    scores = tiles * all_blocks + indices
    rank = jnp.sum((scores[None, :] > scores[:, None]).astype(jnp.int32), axis=1)
    round_ids = rank // owners
    within = rank % owners
    owner_ids = jnp.where(round_ids % 2 == 0, within, owners - 1 - within)
    target = owner_ids * blocks + round_ids
    hit = (target[None, :] == indices[:, None]).astype(jnp.int32)
    source_of = jnp.sum(hit * indices[None, :], axis=1)
    place_tiles = jnp.sum(hit * tiles[None, :], axis=1)
    block_half = indices // half_blocks
    crossing = (owner_ids // quads != block_half).astype(jnp.int32)
    before = (indices[None, :] < indices[:, None]) & (block_half[None, :] == block_half[:, None])
    before = before.astype(jnp.int32)
    source_half = source_of // half_blocks
    far = (source_half != block_half).astype(jnp.int32)

    cross_ats, origins, to_ats = ([], [], [])
    needs = []
    for chunk in range(2):
        table = unit_table(chunk, layers)
        units = sum(jnp.where(tiles == 4 + level, table[level], 0) for level in range(CLASSES))
        place_units = jnp.sum(hit * units[None, :], axis=1)
        cross_at = jnp.sum(before * (crossing * units)[None, :], axis=1)
        cross_need = jnp.max(cross_at + crossing * units)
        pair = place_units.reshape(owners, blocks)
        deliver_need = jnp.max(jnp.sum(pair, axis=1))
        origin = jnp.where(
            far == 1, jnp.sum(hit * cross_at[None, :], axis=1), source_of % half_blocks
        )
        to_at = jnp.stack([jnp.zeros((owners,), jnp.int32), pair[:, 0]], axis=1).reshape(-1)
        cross_ats.append(cross_at)
        origins.append(origin)
        to_ats.append(to_at)
        needs.append((cross_need, deliver_need))
    plan = jnp.stack([tiles, crossing, *cross_ats, place_tiles, far, *origins, *to_ats])
    plan = lax.dynamic_slice_in_dim(plan, half * half_blocks, half_blocks, 1).reshape(-1)

    ids = jnp.stack([core, quad, home * blocks + core]).astype(jnp.int32)
    strips0, strips1, polys, lower = new_root(statistics, warm_roots, orders, ids, layers)

    def to_group(strips):
        return lax.all_to_all(strips, ("quad", "rep"), split_axis=0, concat_axis=0, tiled=True)

    spread0 = to_group(strips0)
    strips1 = rest_of_root(strips1, polys, lower, orders, ids, layers)

    fulls = [unit_table(chunk, layers)[-1] for chunk in range(2)]
    one_layer = [unit_table(chunk, 1)[-1] for chunk in range(2)]

    def scaled(units, factor):
        return [-(-units[chunk] * factor * fulls[chunk] // one_layer[chunk]) for chunk in range(2)]

    levels = [
        ([-(-units // SUBS) for units in scaled(cross, half_blocks)], scaled(delivery, 1))
        for cross, delivery in LEVELS
    ]
    levels.append(([half_blocks * full for full in fulls], [2 * full for full in fulls]))

    def make_route(cross_caps, deliver_caps):
        def route(spread0, strips1):
            def swap(array):
                return lax.ppermute(array, "rep", [(0, 1), (1, 0)])

            def across(packed):
                return lax.ppermute(packed, "half", [(0, 1), (1, 0)])

            def deliver(packed):
                return lax.all_to_all(packed, "quad", split_axis=0, concat_axis=0, tiled=True)

            packed0 = pack_cross(spread0, plan, 0, layers, cross_caps[0])
            packed0, strips1 = lax.optimization_barrier((packed0, strips1))
            crossed0 = across(packed0)
            spread1 = to_group(strips1)
            packed1 = pack_cross(spread1, plan, 1, layers, cross_caps[1])
            crossed1 = across(packed1)
            crossed0, _ = lax.optimization_barrier((crossed0, packed1))
            own0 = deliver(pack_deliver(spread0, crossed0, plan, 0, layers, deliver_caps[0]))
            packed1 = pack_deliver(spread1, crossed1, plan, 1, layers, deliver_caps[1])
            own0, packed1 = lax.optimization_barrier((own0, packed1))
            own1 = deliver(packed1)
            begun = assemble(own0, swap(own0), plan, ids, 0, layers)
            own1, begun = lax.optimization_barrier((own1, begun))
            return assemble(own1, swap(own1), plan, ids, 1, layers, begun)

        return route

    level = jnp.int32(0)
    for caps in levels[:-1]:
        short = jnp.bool_(False)
        for chunk in range(2):
            for which in range(2):
                short = short | (needs[chunk][which] > caps[which][chunk])
        level = level + short.astype(jnp.int32)
    routes = [make_route(*caps) for caps in levels]
    result = lax.switch(level, routes, spread0, strips1)
    return result.reshape(blocks, order_pad, order_pad)


def solution(mesh):
    owners, replicas = (mesh.shape["fsdp"], mesh.shape["rep"])
    devices = np.asarray(mesh.devices).reshape(2, owners // 2, replicas)
    halves = Mesh(devices, ("half", "quad", "rep"))
    whole = P(("half", "quad"), None, None)
    return jax.shard_map(
        on_device, mesh=halves, in_specs=(whole, whole, P()), out_specs=whole, check_vma=False
    )
```

```python
import functools
import math

import jax
import jax.numpy as jnp
import numpy as np
from jax import lax
from jax.experimental import pallas as pl
from jax.experimental.pallas import tpu as pltpu
from jax.sharding import Mesh
from jax.sharding import PartitionSpec as P

CLASSES = 5
SUBS = 16
LANES = 128
ROW_BAND, COL_BAND = (512, 1024)
F_ROOT = 0.2720217172
F_CONST = 0.8666936427
G_CONST = 1.4422628010
G_LIN = -0.4526706801
G_SQ = -1.5220217172
FIRST_ROWS = {4: 2, 5: 3, 6: 3, 7: 3, 8: 4}
LEVELS = (
    ((145, 156), (47, 47)),
    ((170, 182), (47, 47)),
    ((195, 209), (47, 47)),
    ((230, 246), (56, 56)),
    ((285, 305), (56, 56)),
)


def chunk_rows(tiles, chunk):
    first = FIRST_ROWS[tiles]
    return (0, first) if chunk == 0 else (first, tiles - first)


def strip_units(tiles, chunk, layers):
    count = chunk_rows(tiles, chunk)[1]
    return -(-count // layers) * tiles


def unit_table(chunk, layers):
    return [strip_units(4 + level, chunk, layers) for level in range(CLASSES)]


def lanes(start, units):
    return pl.ds(pl.multiple_of(start * LANES, LANES), units * LANES)


def any_spec():
    return pl.BlockSpec(memory_space=pl.ANY)


def vmem_spec():
    return pl.BlockSpec(memory_space=pltpu.VMEM)


def smem_spec():
    return pl.BlockSpec(memory_space=pltpu.SMEM)


SCHEDULE_FLOPS = 3 * 10**10


def cost(moved, flops=0):
    return pl.CostEstimate(flops=flops, bytes_accessed=moved, transcendentals=0)


def loop(first, stop, body):
    lax.fori_loop(first, stop, lambda index, _: body(index), None)


def both_passes(run):
    run(lambda copy: copy.start())
    run(lambda copy: copy.wait())


def for_class(tiles, body):
    for level in range(CLASSES):
        pl.when(tiles == 4 + level)(functools.partial(body, 4 + level))


def split(value):
    high = value.astype(jnp.bfloat16)
    return high, (value - high.astype(jnp.float32)).astype(jnp.bfloat16)


def store_rows(source, outs, tiles, span, layers, sems):
    tiled = source.reshape(-1, SUBS, 8, source.shape[1])

    def run(act):
        def store(count):
            for chunk in range(2):
                begin, rows = chunk_rows(count, chunk)

                def one_row(row, begin=begin, chunk=chunk):
                    layer = pl.multiple_of(lax.rem(row - begin, layers) * SUBS, SUBS)
                    act(
                        pltpu.make_async_copy(
                            tiled.at[row - span.start, :, :, pl.ds(0, count * LANES)],
                            outs[chunk].at[
                                pl.ds(layer, SUBS), :, lanes((row - begin) // layers * count, count)
                            ],
                            sems.at[row],
                        )
                    )

                low, high = (max(begin, span.start), min(begin + rows, span.stop))
                if low < high:
                    loop(low, high, one_row)

        for_class(tiles, store)

    both_passes(run)


def split_dot(left, right, rows, view):
    def part(i, j):
        return jnp.dot(left[i, rows, :], right[j, :, view], preferred_element_type=jnp.float32)

    return part(0, 0) + part(0, 1) + part(1, 0)


def new_root(statistics, warm_roots, orders, ids, layers):
    size = statistics.shape[1]
    tile, half = (size // 8, size // 2)

    def kernel(ids_ref, orders_ref, stat_ref, warm_ref, out0, out1, polys_out, warm_out, *scratch):
        full0, full1, warm, stat, first, second, third, load_sems, store_sems, keep_sems = scratch
        core = ids_ref[0]
        order = orders_ref[ids_ref[2]]
        tiles = order // tile

        def load(source, target, which):
            return [
                pltpu.make_async_copy(
                    source.at[core, pl.ds(row * tile, tile), :],
                    target.at[pl.ds(row * tile, tile), :],
                    load_sems.at[which, row],
                )
                for row in range(8)
            ]

        load_warm = load(warm_ref, full0, 0)
        load_stat = load(stat_ref, full1, 1)
        for copy in load_warm:
            copy.start()

        def keep(pair, rows, view, value):
            high, low = split(value)
            pair[0, rows, view] = high
            pair[1, rows, view] = low

        live_cols = jnp.where(lax.broadcasted_iota(jnp.int32, (1, size), 1) < order, 1.0, 0.0)

        every = slice(0, size)

        def live_rows(rows):
            row_ids = lax.broadcasted_iota(jnp.int32, (rows.size, 1), 0) + rows.start
            return jnp.where(row_ids < order, 1.0, 0.0)

        def take_live(source, pair, row):
            rows = pl.ds(row * tile, tile)
            live = live_cols * jnp.where(row < tiles, 1.0, 0.0)
            keep(pair, rows, slice(0, size), source[rows, :] * live)

        def each(body):
            def step(index, _):
                rows = pl.ds(pl.multiple_of(index * ROW_BAND, ROW_BAND), ROW_BAND)
                for at in range(0, size, COL_BAND):
                    body(rows, slice(at, at + COL_BAND))

            lax.fori_loop(0, size // ROW_BAND, step, None)

        def add_diagonal(source, pair, scale):
            def step(index, _):
                at = pl.multiple_of(index * tile, tile)
                view = pl.ds(at, tile)
                row_ids = lax.broadcasted_iota(jnp.int32, (tile, tile), 0)
                col_ids = lax.broadcasted_iota(jnp.int32, (tile, tile), 1)
                on = (row_ids == col_ids) & (index < tiles)
                value = source[view, view] + jnp.where(on, scale, 0.0)
                source[view, view] = value
                keep(pair, view, view, value)

            lax.fori_loop(0, 8, step, None)

        for row in range(8):
            load_warm[row].wait()
            take_live(full0, warm, row)
        for copy in load_stat:
            copy.start()
        each(lambda rows, view: keep(first, rows, view, split_dot(warm, warm, rows, view)))
        for copy in load_stat:
            copy.wait()

        def make_fourth(rows, view):
            keep(second, rows, view, split_dot(first, first, rows, view))
            at = view.start // COL_BAND * (ROW_BAND * COL_BAND // size)
            some = pl.ds(rows.start + at, ROW_BAND * COL_BAND // size)
            live = live_cols * live_rows(some)
            keep(stat, some, every, full1[some, :] * live)

        each(make_fourth)

        def make_factor(rows, view):
            value = split_dot(second, stat, rows, view) * -0.25
            full0[rows, view] = value
            keep(first, rows, view, value)

        each(make_factor)
        add_diagonal(full0, first, 1.25)

        def make_square(rows, view):
            value = split_dot(first, first, rows, view)
            full1[rows, view] = value
            keep(third, rows, view, value)

        each(make_square)

        def make_polynomials(rows, view):
            cube = split_dot(third, first, rows, view)
            factor, square = (full0[rows, view], full1[rows, view])
            keep(second, rows, view, cube + F_ROOT * square + F_CONST * factor)
            value = cube + G_SQ * square + G_LIN * factor
            full1[rows, view] = value
            keep(stat, rows, view, value)

        each(make_polynomials)
        add_diagonal(full1, stat, G_CONST)
        kept = [
            pltpu.make_async_copy(second, polys_out.at[0], keep_sems.at[0]),
            pltpu.make_async_copy(stat, polys_out.at[1], keep_sems.at[1]),
            pltpu.make_async_copy(warm.at[:, pl.ds(half, half), :], warm_out, keep_sems.at[2]),
        ]
        for save in kept:
            save.start()
        upper = slice(0, half)
        keep(first, upper, every, split_dot(warm, second, upper, every))
        full0[upper, :] = split_dot(first, stat, upper, every)
        store_rows(full0, (out0, out1), tiles, range(0, 4), layers, store_sems)
        for save in kept:
            save.wait()

    pair = pltpu.VMEM((2, size, size), jnp.bfloat16)
    return pl.pallas_call(
        kernel,
        out_shape=[
            jax.ShapeDtypeStruct((SUBS * layers, 8, unit_table(chunk, layers)[-1] * LANES), jnp.float32)
            for chunk in range(2)
        ]
        + [
            jax.ShapeDtypeStruct((2, 2, size, size), jnp.bfloat16),
            jax.ShapeDtypeStruct((2, half, size), jnp.bfloat16),
        ],
        in_specs=[smem_spec()] * 2 + [any_spec()] * 2,
        out_specs=[any_spec()] * 4,
        scratch_shapes=[pltpu.VMEM((size, size), jnp.float32)] * 2
        + [pair] * 5
        + [pltpu.SemaphoreType.DMA((2, 8)), pltpu.SemaphoreType.DMA((8,)), pltpu.SemaphoreType.DMA((3,))],
        compiler_params=pltpu.CompilerParams(vmem_limit_bytes=56 * 2**20),
        cost_estimate=cost(20 * size * size, 36 * size**3),
        name="new_root",
    )(ids, orders, statistics, warm_roots)


def rest_of_root(strips, polys, warm, orders, ids, layers):
    half, size = warm.shape[1:]

    def kernel(ids_ref, orders_ref, _, polys_ref, warm_ref, out_ref, *scratch):
        poly, left, right, product, load_sems, store_sems = scratch
        loads = [
            pltpu.make_async_copy(warm_ref, left, load_sems.at[0]),
            pltpu.make_async_copy(polys_ref.at[0], poly.at[0], load_sems.at[1]),
            pltpu.make_async_copy(polys_ref.at[1], poly.at[1], load_sems.at[2]),
        ]
        for load in loads:
            load.start()
        every = slice(0, size)
        rows = slice(0, half)
        loads[0].wait()
        loads[1].wait()
        high, low = split(split_dot(left, poly.at[0], rows, every))
        right[0] = high
        right[1] = low
        loads[2].wait()
        product[...] = split_dot(right, poly.at[1], rows, every)
        tiles = orders_ref[ids_ref[2]] // (size // 8)
        store_rows(product, (None, out_ref), tiles, range(4, 8), layers, store_sems)

    part = pltpu.VMEM((2, half, size), jnp.bfloat16)
    return pl.pallas_call(
        kernel,
        out_shape=jax.ShapeDtypeStruct(strips.shape, strips.dtype),
        in_specs=[smem_spec()] * 2 + [any_spec()] * 3,
        out_specs=any_spec(),
        scratch_shapes=[pltpu.VMEM((2, 2, size, size), jnp.bfloat16), part, part]
        + [pltpu.VMEM((half, size), jnp.float32)]
        + [pltpu.SemaphoreType.DMA((3,)), pltpu.SemaphoreType.DMA((8,))],
        input_output_aliases={2: 0},
        compiler_params=pltpu.CompilerParams(vmem_limit_bytes=40 * 2**20),
        cost_estimate=cost(12 * size * size, 6 * size**3),
        name="rest_of_root",
    )(ids, orders, strips, polys, warm)


TILES, CROSSING, CROSS_AT, PLACE_TILES, FAR, ORIGIN, TO_AT, PLAN_ROWS = 0, 1, 2, 4, 5, 6, 8, 10


def pack_cross(spread, plan, chunk, layers, capacity):
    blocks = spread.shape[0]

    def kernel(plan_ref, spread_ref, out_ref, sems):
        def copy(block, count):
            units = strip_units(count, chunk, layers)
            start = plan_ref[(CROSS_AT + chunk) * blocks + block]
            return pltpu.make_async_copy(
                spread_ref.at[block, :, pl.ds(0, units * LANES)],
                out_ref.at[:, lanes(start, units)],
                sems.at[block],
            )

        def run(act):
            def each(block):
                @pl.when(plan_ref[CROSSING * blocks + block] == 1)
                def _():
                    tiles = plan_ref[TILES * blocks + block]
                    for_class(tiles, lambda count: act(copy(block, count)))

            loop(0, blocks, each)

        both_passes(run)

    return pl.pallas_call(
        kernel,
        out_shape=jax.ShapeDtypeStruct((8, capacity * LANES), jnp.float32),
        in_specs=[smem_spec(), vmem_spec()],
        out_specs=any_spec(),
        scratch_shapes=[pltpu.SemaphoreType.DMA((blocks,))],
        cost_estimate=cost(4 * spread.size + 32 * capacity * LANES, SCHEDULE_FLOPS),
        name=f"pack_cross_{chunk}",
    )(plan, spread)


def pack_deliver(spread, crossed, plan, chunk, layers, capacity):
    places = spread.shape[0]

    def kernel(plan_ref, spread_ref, crossed_ref, out_ref, sems):
        def copy(place, count, from_far):
            units = strip_units(count, chunk, layers)
            source = plan_ref[(ORIGIN + chunk) * places + place]
            target = plan_ref[(TO_AT + chunk) * places + place]
            if from_far:
                origin = crossed_ref.at[:, lanes(source, units)]
            else:
                origin = spread_ref.at[source, :, pl.ds(0, units * LANES)]
            return pltpu.make_async_copy(
                origin, out_ref.at[place // 2, :, lanes(target, units)], sems.at[place]
            )

        def run(act):
            def each(place):
                for from_far in range(2):

                    @pl.when(plan_ref[FAR * places + place] == from_far)
                    def _(from_far=from_far):
                        tiles = plan_ref[PLACE_TILES * places + place]
                        for_class(tiles, lambda count: act(copy(place, count, from_far == 1)))

            loop(0, places, each)

        both_passes(run)

    return pl.pallas_call(
        kernel,
        out_shape=jax.ShapeDtypeStruct((places // 2, 8, capacity * LANES), jnp.float32),
        in_specs=[smem_spec()] + [vmem_spec()] * 2,
        out_specs=any_spec(),
        scratch_shapes=[pltpu.SemaphoreType.DMA((places,))],
        cost_estimate=cost(4 * (spread.size + crossed.size) + 16 * places * capacity * LANES, SCHEDULE_FLOPS),
        name=f"pack_deliver_{chunk}",
    )(plan, spread, crossed)


def assemble(own, other, plan, ids, chunk, layers, begun=None):
    per_layer = SUBS // 2
    places = plan.shape[0] // PLAN_ROWS
    shape = (2, 8, per_layer, 2, 8, 8 * LANES)

    def kernel(plan_ref, ids_ref, own_ref, other_ref, *rest):
        if chunk == 0:
            out_ref, zeros, sems, fill_sems = rest
            zeros[...] = jnp.zeros_like(zeros)
        else:
            _, out_ref, sems = rest
        core = ids_ref[0]

        def copy(block, count, row, side):
            first = chunk_rows(count, chunk)[0]
            base = plan_ref[(TO_AT + chunk) * places + ids_ref[1] * 2 + block]
            layer = pl.multiple_of(lax.rem(row, layers) * per_layer, per_layer)
            return pltpu.make_async_copy(
                (own_ref, other_ref)[side].at[
                    pl.ds(layer, per_layer), :, lanes(base + row // layers * count, count)
                ],
                out_ref.at[
                    block, first + row, :, core if side == 0 else 1 - core, :, pl.ds(0, count * LANES)
                ],
                sems.at[block, side, row],
            )

        def fill(block, row, begin):
            view = pl.ds(begin * LANES, (8 - begin) * LANES)
            return pltpu.make_async_copy(
                zeros.at[:, :, :, view],
                out_ref.at[block, row, :, :, :, view],
                fill_sems.at[block, row],
            )

        def run(act):
            def each(block):
                def body(count):
                    def one_row(row):
                        act(copy(block, count, row, 0))
                        act(copy(block, count, row, 1))

                    loop(0, chunk_rows(count, chunk)[1], one_row)
                    if chunk == 0 and count < 8:
                        loop(0, count, lambda row: act(fill(block, row, count)))
                        loop(count, 8, lambda row: act(fill(block, row, 0)))

                for_class(plan_ref[PLACE_TILES * places + ids_ref[1] * 2 + block], body)

            loop(0, 2, each)

        both_passes(run)

    scratch = [pltpu.SemaphoreType.DMA((2, 2, 8))]
    if chunk == 0:
        scratch = [pltpu.VMEM(shape[2:], jnp.float32)] + scratch + [pltpu.SemaphoreType.DMA((2, 8))]
    more = [] if begun is None else [begun]
    return pl.pallas_call(
        kernel,
        out_shape=jax.ShapeDtypeStruct(shape, jnp.float32),
        in_specs=[smem_spec()] * 2 + [vmem_spec()] * 2 + [any_spec()] * len(more),
        out_specs=any_spec(),
        scratch_shapes=scratch,
        input_output_aliases={4: 0} if more else {},
        cost_estimate=cost(4 * (own.size + other.size + math.prod(shape) // 2)),
        name=f"assemble_{chunk}",
    )(plan, ids, own, other, *more)


def on_device(statistics, warm_roots, orders):
    blocks, order_pad = (statistics.shape[0], statistics.shape[1])
    quads = lax.axis_size("quad")
    owners = 2 * quads
    all_blocks = orders.shape[0]
    half_blocks = all_blocks // 2
    layers = owners // SUBS
    half = lax.axis_index("half")
    quad = lax.axis_index("quad")
    core = lax.axis_index("rep")
    home = half * quads + quad
    tile = order_pad // 8

    tiles = orders // tile
    indices = jnp.arange(all_blocks, dtype=jnp.int32)
    scores = tiles * all_blocks + indices
    rank = jnp.sum((scores[None, :] > scores[:, None]).astype(jnp.int32), axis=1)
    round_ids = rank // owners
    within = rank % owners
    owner_ids = jnp.where(round_ids % 2 == 0, within, owners - 1 - within)
    target = owner_ids * blocks + round_ids
    hit = (target[None, :] == indices[:, None]).astype(jnp.int32)
    source_of = jnp.sum(hit * indices[None, :], axis=1)
    place_tiles = jnp.sum(hit * tiles[None, :], axis=1)
    block_half = indices // half_blocks
    crossing = (owner_ids // quads != block_half).astype(jnp.int32)
    before = (indices[None, :] < indices[:, None]) & (block_half[None, :] == block_half[:, None])
    before = before.astype(jnp.int32)
    source_half = source_of // half_blocks
    far = (source_half != block_half).astype(jnp.int32)

    cross_ats, origins, to_ats = ([], [], [])
    needs = []
    for chunk in range(2):
        table = unit_table(chunk, layers)
        units = sum(jnp.where(tiles == 4 + level, table[level], 0) for level in range(CLASSES))
        place_units = jnp.sum(hit * units[None, :], axis=1)
        cross_at = jnp.sum(before * (crossing * units)[None, :], axis=1)
        cross_need = jnp.max(cross_at + crossing * units)
        pair = place_units.reshape(owners, blocks)
        deliver_need = jnp.max(jnp.sum(pair, axis=1))
        origin = jnp.where(
            far == 1, jnp.sum(hit * cross_at[None, :], axis=1), source_of % half_blocks
        )
        to_at = jnp.stack([jnp.zeros((owners,), jnp.int32), pair[:, 0]], axis=1).reshape(-1)
        cross_ats.append(cross_at)
        origins.append(origin)
        to_ats.append(to_at)
        needs.append((cross_need, deliver_need))
    plan = jnp.stack([tiles, crossing, *cross_ats, place_tiles, far, *origins, *to_ats])
    plan = lax.dynamic_slice_in_dim(plan, half * half_blocks, half_blocks, 1).reshape(-1)

    ids = jnp.stack([core, quad, home * blocks + core]).astype(jnp.int32)
    strips0, strips1, polys, lower = new_root(statistics, warm_roots, orders, ids, layers)

    def to_group(strips):
        return lax.all_to_all(strips, ("quad", "rep"), split_axis=0, concat_axis=0, tiled=True)

    spread0 = to_group(strips0)
    strips1 = rest_of_root(strips1, polys, lower, orders, ids, layers)

    fulls = [unit_table(chunk, layers)[-1] for chunk in range(2)]
    one_layer = [unit_table(chunk, 1)[-1] for chunk in range(2)]

    def scaled(units, factor):
        return [-(-units[chunk] * factor * fulls[chunk] // one_layer[chunk]) for chunk in range(2)]

    levels = [
        ([-(-units // SUBS) for units in scaled(cross, half_blocks)], scaled(delivery, 1))
        for cross, delivery in LEVELS
    ]
    levels.append(([half_blocks * full for full in fulls], [2 * full for full in fulls]))

    def make_route(cross_caps, deliver_caps):
        def route(spread0, strips1):
            def swap(array):
                return lax.ppermute(array, "rep", [(0, 1), (1, 0)])

            def across(packed):
                return lax.ppermute(packed, "half", [(0, 1), (1, 0)])

            def deliver(packed):
                return lax.all_to_all(packed, "quad", split_axis=0, concat_axis=0, tiled=True)

            packed0 = pack_cross(spread0, plan, 0, layers, cross_caps[0])
            crossed0 = across(packed0)
            spread1 = to_group(strips1)
            packed1 = pack_cross(spread1, plan, 1, layers, cross_caps[1])
            crossed1 = across(packed1)
            crossed0, _ = lax.optimization_barrier((crossed0, packed1))
            own0 = deliver(pack_deliver(spread0, crossed0, plan, 0, layers, deliver_caps[0]))
            packed1 = pack_deliver(spread1, crossed1, plan, 1, layers, deliver_caps[1])
            own0, packed1 = lax.optimization_barrier((own0, packed1))
            own1 = deliver(packed1)
            begun = assemble(own0, swap(own0), plan, ids, 0, layers)
            own1, begun = lax.optimization_barrier((own1, begun))
            return assemble(own1, swap(own1), plan, ids, 1, layers, begun)

        return route

    level = jnp.int32(0)
    for caps in levels[:-1]:
        short = jnp.bool_(False)
        for chunk in range(2):
            for which in range(2):
                short = short | (needs[chunk][which] > caps[which][chunk])
        level = level + short.astype(jnp.int32)
    routes = [make_route(*caps) for caps in levels]
    result = lax.switch(level, routes, spread0, strips1)
    return result.reshape(blocks, order_pad, order_pad)


def solution(mesh):
    owners, replicas = (mesh.shape["fsdp"], mesh.shape["rep"])
    devices = np.asarray(mesh.devices).reshape(2, owners // 2, replicas)
    halves = Mesh(devices, ("half", "quad", "rep"))
    whole = P(("half", "quad"), None, None)
    return jax.shard_map(
        on_device, mesh=halves, in_specs=(whole, whole, P()), out_specs=whole, check_vma=False
    )
```
